32 devices in a mesh: groups: 2 (over y), dp: 4 (over z), tensor: 4 (over x, core).
Axes of the slice: x: 2, y: 2, z: 4, core: 2. Of those that a mesh axis runs over, the one named last changes fastest.
Arguments:
- acts: bfloat16 [64, 128, 8192], P(('groups', 'dp'), None, 'tensor'), parts along dimension 0, may hold values from -6 to 6
- grads: bfloat16 [64, 128, 8192], P(('groups', 'dp'), None, 'tensor'), parts along dimension 0, may hold values from -6 to 6
- basis_in: bfloat16 [64, 8192], P(None, 'tensor'), may hold values from -0.0625 to 0.0625
- basis_out: bfloat16 [64, 8192], P(None, 'tensor'), may hold values from -0.0625 to 0.0625
- queries: bfloat16 [512, 4096], P(('groups', 'dp')), parts along dimension 0, may hold values from -6 to 6
Outputs:
- scores: float32 [64, 256], P(('groups', 'dp', 'tensor')), parts along dimension 0
The draws below stay inside these ranges and needn't reach their ends.
There are 2 independent parts, one for each index of `groups`. The reference program is written for one: setup_inputs(seed, part) draws one part's arguments, and reference() takes and returns one part's arrays. A program takes and returns all parts, laid end to end along the dimension named above; an argument that names none is the same for every part. Nothing has to cross between parts.
All inputs are finite; a program needn't handle non-finite values.
Results may differ from the reference program's by a relative error of at most 0.003.
Values may be sent and summed in bfloat16 or wider, within the bound.
No kernel may reach another device: no remote copies, remote signals or barrier semaphores. Data moves between devices by JAX's collectives and lax.ppermute only.
A program may use at most 64 MiB of HBM per device.

```python
import jax
import jax.numpy as jnp
from jax import lax

HID = 8192
RANK = 64
LEN = 128
SKETCH = 4096
TRAIN_SEQ = 32
QUERIES = 256


def block_scale(key, dims, split, low, top_value):
    factor_of = 1.0
    for position, parts in split:
        steps = jax.random.uniform(jax.random.fold_in(jax.random.fold_in(key, 6), position), (parts,), jnp.float32, low / len(split), top_value / len(split))
        factor_of = factor_of * jnp.repeat(jnp.exp(steps), dims[position] // parts).reshape((-1,) + (1,) * (len(dims) - 1 - position))
    return factor_of


def gaussian(key, extent, spread, reach, cuts=(), kind=jnp.bfloat16):
    result = jax.random.normal(key, extent, jnp.float32) * spread
    if len(cuts) > 0:
        result = block_scale(key, extent, cuts, -0.22, 0.18) * result
    return jnp.clip(result, min=-reach, max=reach).astype(kind)


def setup_inputs(seed: int = 0, part: int = 0) -> dict:
    seeds = jax.random.split(jax.random.key(seed), 6)
    part_keys = jax.random.split(jax.random.fold_in(seeds[5], part), 6)
    acts = gaussian(part_keys[0], (TRAIN_SEQ, LEN, HID), 1.0, 6.0, ((0, 4), (2, 4)))
    grads = gaussian(part_keys[1], (TRAIN_SEQ, LEN, HID), 1.0, 6.0, ((0, 4), (2, 4)))
    basis_in = gaussian(seeds[2], (RANK, HID), HID ** -0.5, 0.0625, ((1, 4),))
    basis_out = gaussian(seeds[3], (RANK, HID), HID ** -0.5, 0.0625, ((1, 4),))
    queries = gaussian(part_keys[4], (QUERIES, SKETCH), 1.0, 6.0, ((0, 4),))
    return dict(acts=acts, grads=grads, basis_in=basis_in, basis_out=basis_out, queries=queries)


def one_sketch(pair, basis_in, basis_out):
    inputs, outgrads = pair
    left = jnp.dot(inputs, basis_in.T, preferred_element_type=jnp.float32)
    right = jnp.dot(outgrads, basis_out.T, preferred_element_type=jnp.float32)
    outer = jnp.dot(left.T, right, precision=lax.Precision.HIGHEST) / LEN
    return outer.reshape(SKETCH).astype(jnp.bfloat16)


def reference(acts, grads, basis_in, basis_out, queries):
    sketch = lax.map(lambda pair: one_sketch(pair, basis_in, basis_out), (acts, grads))
    return jnp.dot(sketch, queries.T, preferred_element_type=jnp.float32) / RANK
```

```python
import jax
import jax.numpy as jnp
from jax import lax
from jax.sharding import PartitionSpec as P

BF, F32 = jnp.bfloat16, jnp.float32


def local(acts, grads, basis_in, basis_out, queries):
    rank = basis_in.shape[0]
    length = acts.shape[1]
    nt, nd = lax.axis_size("tensor"), lax.axis_size("dp")
    nx, no = nt // 2, nd // 2
    t, d = lax.axis_index("tensor"), lax.axis_index("dp")
    x, c = t // 2, t % 2
    o, i = d // 2, d % 2
    own = acts.shape[0] // nt
    nq = queries.shape[0]
    core = [(k, k ^ 1) for k in range(nt)]

    def xshift(k):
        return [(a * 2 + b, ((a + k) % nx) * 2 + b) for a in range(nx) for b in range(2)]

    def oshift(k):
        return [(a * 2 + b, ((a + k) % no) * 2 + b) for a in range(no) for b in range(2)]

    near = [(k, k ^ 1) for k in range(nd)]

    half = nq // 2
    part = lax.dynamic_slice_in_dim(queries, c * half, half, 0)
    far_mine = lax.ppermute(part, "dp", near)
    far_other = lax.ppermute(far_mine, "tensor", core)

    left = jnp.einsum("slh,rh->slr", acts, basis_in, preferred_element_type=F32)
    right = jnp.einsum("slh,rh->slr", grads, basis_out, preferred_element_type=F32)
    joined = jnp.concatenate([left, right], axis=2).reshape(nx, 2, own, length, 2 * rank)
    give = lax.dynamic_index_in_dim(joined, 1 - c, 1, False)
    keep = lax.dynamic_index_in_dim(joined, c, 1, False)
    keep = keep + lax.ppermute(give, "tensor", core)
    mine = lax.dynamic_index_in_dim(keep, x, 0, False)
    for k in range(1, nx):
        give = lax.dynamic_index_in_dim(keep, (x + k) % nx, 0, False).astype(BF)
        mine = mine + lax.ppermute(give, "tensor", xshift(k)).astype(F32)
    outer = jnp.einsum("slr,slq->srq", mine[:, :, :rank], mine[:, :, rank:], precision=lax.Precision.HIGHEST)
    sketch = outer.reshape(own, rank * rank) / (length * rank)

    hi = sketch.astype(BF)
    lo = (sketch - hi.astype(F32)).astype(BF)
    rows = jnp.concatenate([hi, lo], 0)
    all_rows = [rows] + [lax.ppermute(rows, "dp", oshift(k)) for k in range(1, no)]
    stacked = jnp.concatenate(all_rows, 0)

    def score(q):
        s = lax.dot_general(stacked, q, (((1,), (1,)), ((), ())), preferred_element_type=F32)
        s = s.reshape(no, 2, own, -1)
        return s[:, 0] + s[:, 1]

    near_s = score(queries)
    fm, fo = score(far_mine), score(far_other)
    lohalf, hihalf = jnp.where(c == 0, fm, fo), jnp.where(c == 0, fo, fm)
    far_s = jnp.concatenate([lohalf, hihalf], 2)
    first = jnp.where(i == 0, near_s, far_s)
    second = jnp.where(i == 0, far_s, near_s)
    both = jnp.concatenate([first, second], 2)
    blocks = [both[0]] + [lax.ppermute(both[k], "dp", oshift(no - k)) for k in range(1, no)]
    allb = jnp.stack(blocks, 0)
    allb = jnp.roll(allb, o, axis=0) if no > 2 else jnp.where(o == 0, allb, allb[::-1])
    return jnp.swapaxes(allb, 0, 1).reshape(own, nd * nq)


def solution(mesh):
    in_specs = (
        P(("groups", "dp"), None, "tensor"),
        P(("groups", "dp"), None, "tensor"),
        P(None, "tensor"),
        P(None, "tensor"),
        P(("groups", "dp"), None),
    )
    out_specs = P(("groups", "dp", "tensor"), None)
    return jax.shard_map(local, mesh=mesh, in_specs=in_specs, out_specs=out_specs, check_vma=False)
```

```python
import functools

import jax
import jax.numpy as jnp
from jax import lax
from jax.experimental import pallas as pl
from jax.experimental.pallas import tpu as pltpu
from jax.sharding import PartitionSpec as P

BF, F32 = jnp.bfloat16, jnp.float32


def settle_kernel(arrived, held):
    held[...] = arrived[...]


def settle(arrived):
    return pl.pallas_call(
        settle_kernel,
        out_shape=jax.ShapeDtypeStruct(arrived.shape, arrived.dtype),
        in_specs=[pl.BlockSpec(memory_space=pltpu.VMEM)],
        out_specs=pl.BlockSpec(memory_space=pltpu.VMEM),
        compiler_params=pltpu.CompilerParams(vmem_limit_bytes=16 * 2**20),
        cost_estimate=pl.CostEstimate(flops=10000000000, bytes_accessed=0, transcendentals=0),
    )(arrived)


def project_kernel(nx, nt, values, basis, give, keep):
    rows = give.shape[2]
    t = lax.axis_index("tensor")
    x, c = t // 2, t % 2
    for j in range(nt):
        k, other = j % nx, j < nx
        place = lax.rem(x + k, nx) * 2 + ((1 - c) if other else c)
        source = pl.ds(pl.multiple_of(place * rows, rows), rows)
        to = give if other else keep
        to[k] = lax.dot_general(basis[...], values[source], (((1,), (1,)), ((), ())), preferred_element_type=F32)


def project(values, basis, nt):
    rank, hidden = basis.shape
    rows = values.shape[0] // nt
    nx = nt // 2
    shape = jax.ShapeDtypeStruct((nx, rank, rows), F32)
    return pl.pallas_call(
        functools.partial(project_kernel, nx, nt),
        out_shape=[shape, shape],
        in_specs=[pl.BlockSpec(memory_space=pltpu.VMEM)] * 2,
        out_specs=[pl.BlockSpec(memory_space=pltpu.VMEM)] * 2,
        compiler_params=pltpu.CompilerParams(vmem_limit_bytes=16 * 2**20),
        cost_estimate=pl.CostEstimate(flops=2 * nt * rows * hidden * rank, bytes_accessed=2 * nt * rows * hidden, transcendentals=0),
    )(values, basis)


def local(acts, grads, basis_in, basis_out, queries):
    rank = basis_in.shape[0]
    length, hidden = acts.shape[1:]
    nt, nd = lax.axis_size("tensor"), lax.axis_size("dp")
    nx, no = nt // 2, nd // 2
    t, d = lax.axis_index("tensor"), lax.axis_index("dp")
    c = t % 2
    o, i = d // 2, d % 2

    def at(a, b):
        return a * 2 + b

    own = acts.shape[0] // nt
    nq = queries.shape[0]
    core = [(k, k ^ 1) for k in range(nt)]

    def xshift(k):
        return [(a * 2 + b, ((a + k) % nx) * 2 + b) for a in range(nx) for b in range(2)]

    def oshift(k):
        return [(at(a, b), at((a + k) % no, b)) for a in range(no) for b in range(2)]

    near = [(at(a, b), at(a, 1 - b)) for a in range(no) for b in range(2)]

    half, depth = nq // 2, queries.shape[1]
    part = settle(lax.dynamic_slice_in_dim(queries, c * half, half, 0))
    far_mine = lax.ppermute(part, "dp", near)
    acts, grads, part = lax.optimization_barrier((acts, grads, part))

    give_r, keep_r = project(grads.reshape(-1, hidden), basis_out, nt)
    give_l, keep_l = project(acts.reshape(-1, hidden), basis_in, nt)
    got = lax.ppermute(jnp.concatenate([give_l, give_r], 1), "tensor", core)
    keep = jnp.concatenate([keep_l, keep_r], 1) + got
    mine = keep[0]
    groups = [[a * 2 + b for a in range(nx)] for b in range(2)]
    sent = jnp.stack([keep[k] for k in range(1, nx)], 0).astype(BF)
    everyone = lax.all_gather(sent, "tensor", axis=0, axis_index_groups=groups)
    x = t // 2
    for k in range(1, nx):
        mine = mine + lax.dynamic_index_in_dim(everyone, (x - k) % nx, 0, False)[k - 1].astype(F32)
    mine = mine.reshape(2, rank, own, length)
    outer = jnp.einsum("rsl,qsl->srq", mine[0], mine[1], precision=lax.Precision.HIGHEST)
    sketch = outer.reshape(own, rank * rank) / (length * rank)

    top = lax.reduce_precision(sketch, 8, 7)
    hi, lo = top.astype(BF), (sketch - top).astype(BF)
    rows = jnp.concatenate([hi, lo], 0)
    stacked = jnp.concatenate([rows] + [lax.ppermute(rows, "dp", oshift(k)) for k in range(1, no)], 0)
    far_other = lax.ppermute(far_mine, "tensor", core)

    def score(q):
        s = lax.dot_general(stacked, q, (((1,), (1,)), ((), ())), preferred_element_type=F32)
        s = s.reshape(no, 2, own, -1)
        return s[:, 0] + s[:, 1]

    def back(s):
        return [s[0]] + [lax.ppermute(s[k], "dp", oshift(no - k)) for k in range(1, no)]

    near_s = score(queries)
    fm, fo = score(far_mine), score(far_other)
    far_s = jnp.concatenate([jnp.where(c == 0, fm, fo), jnp.where(c == 0, fo, fm)], 2)
    both = jnp.concatenate([jnp.where(i == 0, near_s, far_s), jnp.where(i == 0, far_s, near_s)], 2)
    allb = jnp.stack(back(both), 0)
    allb = jnp.roll(allb, o, axis=0) if no > 2 else jnp.where(o == 0, allb, allb[::-1])
    return jnp.swapaxes(allb, 0, 1).reshape(own, nd * nq)


def solution(mesh):
    in_specs = (
        P(("groups", "dp"), None, "tensor"),
        P(("groups", "dp"), None, "tensor"),
        P(None, "tensor"),
        P(None, "tensor"),
        P(("groups", "dp"), None),
    )
    out_specs = P(("groups", "dp", "tensor"), None)
    return jax.shard_map(local, mesh=mesh, in_specs=in_specs, out_specs=out_specs, check_vma=False)
```

```python
import functools

import jax
import jax.numpy as jnp
from jax import lax
from jax.experimental import pallas as pl
from jax.experimental.pallas import tpu as pltpu
from jax.sharding import PartitionSpec as P

BF, F32 = jnp.bfloat16, jnp.float32


def open_kernel(token):
    token[...] = jnp.zeros_like(token)


def opening():
    return pl.pallas_call(
        open_kernel,
        out_shape=jax.ShapeDtypeStruct((8, 128), F32),
        out_specs=pl.BlockSpec(memory_space=pltpu.VMEM),
        compiler_params=pltpu.CompilerParams(vmem_limit_bytes=16 * 2**20),
        cost_estimate=pl.CostEstimate(flops=10000000000, bytes_accessed=0, transcendentals=0),
    )()


def project_kernel(nx, nt, values, basis, token, give, keep):
    rows = give.shape[2]
    t = lax.axis_index("tensor")
    x, c = t // 2, t % 2
    for j in range(nt):
        k, other = j % nx, j < nx
        place = lax.rem(x + k, nx) * 2 + ((1 - c) if other else c)
        source = pl.ds(pl.multiple_of(place * rows, rows), rows)
        to = give if other else keep
        to[k] = lax.dot_general(basis[...], values[source], (((1,), (1,)), ((), ())), preferred_element_type=F32)


def project(values, basis, token, nt):
    rank, hidden = basis.shape
    rows = values.shape[0] // nt
    nx = nt // 2
    shape = jax.ShapeDtypeStruct((nx, rank, rows), F32)
    return pl.pallas_call(
        functools.partial(project_kernel, nx, nt),
        out_shape=[shape, shape],
        in_specs=[pl.BlockSpec(memory_space=pltpu.VMEM)] * 3,
        out_specs=[pl.BlockSpec(memory_space=pltpu.VMEM)] * 2,
        compiler_params=pltpu.CompilerParams(vmem_limit_bytes=16 * 2**20),
        cost_estimate=pl.CostEstimate(flops=2 * nt * rows * hidden * rank, bytes_accessed=2 * nt * rows * hidden, transcendentals=0),
    )(values, basis, token)


def score_kernel(no, own, outer_axis, rows, near, mine, other, out):
    c = lax.axis_index("tensor") % 2
    d = lax.axis_index("dp")
    i = d % 2 if outer_axis else d // no

    def product(q):
        return lax.dot_general(rows[...], q[...], (((1,), (1,)), ((), ())), preferred_element_type=F32)

    n, m, f = product(near), product(mine), product(other)
    far = jnp.where(c == 0, jnp.concatenate([m, f], 1), jnp.concatenate([f, m], 1))
    every = jnp.where(i == 0, jnp.concatenate([n, far], 1), jnp.concatenate([far, n], 1))
    for k in range(no):
        at = 2 * own * k
        out[k] = every[at : at + own] + every[at + own : at + 2 * own]


def score(rows, near, mine, other, no, own, outer_axis):
    return pl.pallas_call(
        functools.partial(score_kernel, no, own, outer_axis),
        out_shape=jax.ShapeDtypeStruct((no, own, 2 * near.shape[0]), F32),
        in_specs=[pl.BlockSpec(memory_space=pltpu.VMEM)] * 4,
        out_specs=pl.BlockSpec(memory_space=pltpu.VMEM),
        compiler_params=pltpu.CompilerParams(vmem_limit_bytes=16 * 2**20),
        cost_estimate=pl.CostEstimate(flops=4 * rows.size * near.shape[0], bytes_accessed=2 * near.size, transcendentals=0),
    )(rows, near, mine, other)


def local(acts, grads, basis_in, basis_out, queries):
    rank = basis_in.shape[0]
    length, hidden = acts.shape[1:]
    nt, nd = lax.axis_size("tensor"), lax.axis_size("dp")
    nx, no = nt // 2, nd // 2
    t, d = lax.axis_index("tensor"), lax.axis_index("dp")
    c = t % 2
    o, i = d // 2, d % 2

    def at(a, b):
        return a * 2 + b

    own = acts.shape[0] // nt
    nq = queries.shape[0]
    core = [(k, k ^ 1) for k in range(nt)]

    def xshift(k):
        return [(a * 2 + b, ((a + k) % nx) * 2 + b) for a in range(nx) for b in range(2)]

    def oshift(k):
        return [(at(a, b), at((a + k) % no, b)) for a in range(no) for b in range(2)]

    near = [(at(a, b), at(a, 1 - b)) for a in range(no) for b in range(2)]

    half, depth = nq // 2, queries.shape[1]
    part = lax.dynamic_slice_in_dim(queries, c * half, half, 0)
    token = opening()
    far_mine = lax.ppermute(part, "dp", near)

    give_r, keep_r = project(grads.reshape(-1, hidden), basis_out, token, nt)
    give_l, keep_l = project(acts.reshape(-1, hidden), basis_in, token, nt)
    got = lax.ppermute(jnp.concatenate([give_l, give_r], 1), "tensor", core)
    keep = jnp.concatenate([keep_l, keep_r], 1) + got
    mine = keep[0]
    groups = [[a * 2 + b for a in range(nx)] for b in range(2)]
    sent = jnp.stack([keep[k] for k in range(1, nx)], 0).astype(BF)
    everyone = lax.all_gather(sent, "tensor", axis=0, axis_index_groups=groups)
    x = t // 2
    for k in range(1, nx):
        mine = mine + lax.dynamic_index_in_dim(everyone, (x - k) % nx, 0, False)[k - 1].astype(F32)
    mine = mine.reshape(2, rank, own, length)
    outer = jnp.einsum("rsl,qsl->srq", mine[0], mine[1], precision=lax.Precision.HIGHEST)
    sketch = outer.reshape(own, rank * rank) / (length * rank)

    top = lax.reduce_precision(sketch, 8, 7)
    hi, lo = top.astype(BF), (sketch - top).astype(BF)
    rows = jnp.concatenate([hi, lo], 0)
    stacked = jnp.concatenate([rows] + [lax.ppermute(rows, "dp", oshift(k)) for k in range(1, no)], 0)
    far_other = lax.ppermute(far_mine, "tensor", core)

    def back(s):
        return [s[0]] + [lax.ppermute(s[k], "dp", oshift(no - k)) for k in range(1, no)]

    allb = jnp.stack(back(score(stacked, queries, far_mine, far_other, no, own, True)), 0)
    allb = jnp.roll(allb, o, axis=0) if no > 2 else jnp.where(o == 0, allb, allb[::-1])
    return jnp.swapaxes(allb, 0, 1).reshape(own, nd * nq)


def solution(mesh):
    in_specs = (
        P(("groups", "dp"), None, "tensor"),
        P(("groups", "dp"), None, "tensor"),
        P(None, "tensor"),
        P(None, "tensor"),
        P(("groups", "dp"), None),
    )
    out_specs = P(("groups", "dp", "tensor"), None)
    return jax.shard_map(local, mesh=mesh, in_specs=in_specs, out_specs=out_specs, check_vma=False)
```

```python
import functools

import jax
import jax.numpy as jnp
from jax import lax
from jax.experimental import pallas as pl
from jax.experimental.pallas import tpu as pltpu
from jax.sharding import PartitionSpec as P

BF, F32 = jnp.bfloat16, jnp.float32


def open_kernel(token):
    token[...] = jnp.zeros_like(token)


def opening():
    return pl.pallas_call(
        open_kernel,
        out_shape=jax.ShapeDtypeStruct((8, 128), F32),
        out_specs=pl.BlockSpec(memory_space=pltpu.VMEM),
        compiler_params=pltpu.CompilerParams(vmem_limit_bytes=16 * 2**20),
        cost_estimate=pl.CostEstimate(flops=10000000000, bytes_accessed=0, transcendentals=0),
    )()


def project_kernel(nx, nt, values, basis, token, give, keep):
    rows = give.shape[2]
    t = lax.axis_index("tensor")
    x, c = t // 2, t % 2
    for j in range(nt):
        k, other = j % nx, j < nx
        place = lax.rem(x + k, nx) * 2 + ((1 - c) if other else c)
        source = pl.ds(pl.multiple_of(place * rows, rows), rows)
        to = give if other else keep
        to[k] = lax.dot_general(values[source], basis[...], (((1,), (1,)), ((), ())), preferred_element_type=F32).T


def project(values, basis, token, nt):
    rank, hidden = basis.shape
    rows = values.shape[0] // nt
    nx = nt // 2
    shape = jax.ShapeDtypeStruct((nx, rank, rows), F32)
    return pl.pallas_call(
        functools.partial(project_kernel, nx, nt),
        out_shape=[shape, shape],
        in_specs=[pl.BlockSpec(memory_space=pltpu.VMEM)] * 3,
        out_specs=[pl.BlockSpec(memory_space=pltpu.VMEM)] * 2,
        compiler_params=pltpu.CompilerParams(vmem_limit_bytes=16 * 2**20),
        cost_estimate=pl.CostEstimate(flops=2 * nt * rows * hidden * rank, bytes_accessed=2 * nt * rows * hidden, transcendentals=0),
    )(values, basis, token)


def outer_kernel(nx, own, scale, keep, everyone, sketch):
    x = lax.axis_index("tensor") // 2
    mine = keep[0]
    for k in range(1, nx):
        mine = mine + everyone[lax.rem(x + nx - k, nx), k - 1].astype(F32)
    rank, length = mine.shape[0] // 2, mine.shape[1] // own
    for s in range(own):
        part = mine[:, s * length : (s + 1) * length]
        sketch[s] = scale * lax.dot_general(
            part[:rank], part[rank:], (((1,), (1,)), ((), ())), precision=lax.Precision.HIGHEST, preferred_element_type=F32
        )


def outer(keep, everyone, own):
    nx, twice, tokens = keep.shape
    rank = twice // 2
    return pl.pallas_call(
        functools.partial(outer_kernel, nx, own, 1.0 / (tokens // own * rank)),
        out_shape=jax.ShapeDtypeStruct((own, rank, rank), F32),
        in_specs=[pl.BlockSpec(memory_space=pltpu.VMEM)] * 2,
        out_specs=pl.BlockSpec(memory_space=pltpu.VMEM),
        compiler_params=pltpu.CompilerParams(vmem_limit_bytes=16 * 2**20),
        cost_estimate=pl.CostEstimate(flops=12 * rank * rank * tokens, bytes_accessed=4 * keep.size, transcendentals=0),
    )(keep, everyone)


def score_kernel(no, own, outer_axis, rows, near, mine, other, out):
    c = lax.axis_index("tensor") % 2
    value = rows[...]
    hi = value.astype(BF).astype(F32)
    split = jnp.concatenate([hi, value - hi], 0).astype(BF)
    d = lax.axis_index("dp")
    i = d % 2 if outer_axis else d // no

    def product(q):
        return lax.dot_general(split, q[...], (((1,), (1,)), ((), ())), preferred_element_type=F32)

    n, m, f = product(near), product(mine), product(other)
    far = jnp.where(c == 0, jnp.concatenate([m, f], 1), jnp.concatenate([f, m], 1))
    every = jnp.where(i == 0, jnp.concatenate([n, far], 1), jnp.concatenate([far, n], 1))
    for k in range(no):
        out[k] = every[own * k : own * (k + 1)] + every[own * (no + k) : own * (no + k + 1)]


def score(rows, near, mine, other, no, own, outer_axis):
    return pl.pallas_call(
        functools.partial(score_kernel, no, own, outer_axis),
        out_shape=jax.ShapeDtypeStruct((no, own, 2 * near.shape[0]), F32),
        in_specs=[pl.BlockSpec(memory_space=pltpu.VMEM)] * 4,
        out_specs=pl.BlockSpec(memory_space=pltpu.VMEM),
        compiler_params=pltpu.CompilerParams(vmem_limit_bytes=16 * 2**20),
        cost_estimate=pl.CostEstimate(flops=8 * rows.size * near.shape[0], bytes_accessed=2 * near.size, transcendentals=0),
    )(rows, near, mine, other)


def local(acts, grads, basis_in, basis_out, queries):
    rank = basis_in.shape[0]
    length, hidden = acts.shape[1:]
    nt, nd = lax.axis_size("tensor"), lax.axis_size("dp")
    nx, no = nt // 2, nd // 2
    t, d = lax.axis_index("tensor"), lax.axis_index("dp")
    c = t % 2
    o, i = d // 2, d % 2

    def at(a, b):
        return a * 2 + b

    own = acts.shape[0] // nt
    nq = queries.shape[0]
    core = [(k, k ^ 1) for k in range(nt)]

    def xshift(k):
        return [(a * 2 + b, ((a + k) % nx) * 2 + b) for a in range(nx) for b in range(2)]

    def oshift(k):
        return [(at(a, b), at((a + k) % no, b)) for a in range(no) for b in range(2)]

    near = [(at(a, b), at(a, 1 - b)) for a in range(no) for b in range(2)]

    half, depth = nq // 2, queries.shape[1]
    part = lax.dynamic_slice_in_dim(queries, c * half, half, 0)
    token = opening()
    far_mine = lax.ppermute(part, "dp", near)

    give_r, keep_r = project(grads.reshape(-1, hidden), basis_out, token, nt)
    give_l, keep_l = project(acts.reshape(-1, hidden), basis_in, token, nt)
    got = lax.ppermute(jnp.concatenate([give_l, give_r], 1), "tensor", core)
    keep = jnp.concatenate([keep_l, keep_r], 1) + got
    columns = [[a * 2 + b for a in range(nx)] for b in range(2)]
    sent = jnp.stack([keep[k] for k in range(1, nx)], 0).astype(BF)
    everyone = lax.all_gather(sent, "tensor", axis=0, axis_index_groups=columns)
    rows = outer(keep, everyone, own).reshape(own, rank * rank)
    stacked = jnp.concatenate([rows] + [lax.ppermute(rows, "dp", oshift(k)) for k in range(1, no)], 0)
    far_other = lax.ppermute(far_mine, "tensor", core)

    def back(s):
        return [s[0]] + [lax.ppermute(s[k], "dp", oshift(no - k)) for k in range(1, no)]

    allb = jnp.stack(back(score(stacked, queries, far_mine, far_other, no, own, True)), 0)
    allb = jnp.roll(allb, o, axis=0) if no > 2 else jnp.where(o == 0, allb, allb[::-1])
    return jnp.swapaxes(allb, 0, 1).reshape(own, nd * nq)


def solution(mesh):
    in_specs = (
        P(("groups", "dp"), None, "tensor"),
        P(("groups", "dp"), None, "tensor"),
        P(None, "tensor"),
        P(None, "tensor"),
        P(("groups", "dp"), None),
    )
    out_specs = P(("groups", "dp", "tensor"), None)
    return jax.shard_map(local, mesh=mesh, in_specs=in_specs, out_specs=out_specs, check_vma=False)
```

```python
import functools

import jax
import jax.numpy as jnp
from jax import lax
from jax.experimental import pallas as pl
from jax.experimental.pallas import tpu as pltpu
from jax.sharding import PartitionSpec as P

BF, F32 = jnp.bfloat16, jnp.float32


def open_kernel(token):
    token[...] = jnp.zeros_like(token)


def opening():
    return pl.pallas_call(
        open_kernel,
        out_shape=jax.ShapeDtypeStruct((8, 128), F32),
        out_specs=pl.BlockSpec(memory_space=pltpu.VMEM),
        compiler_params=pltpu.CompilerParams(vmem_limit_bytes=16 * 2**20),
        cost_estimate=pl.CostEstimate(flops=10000000000, bytes_accessed=0, transcendentals=0),
    )()


def project_kernel(nx, nt, values, basis, token, give, keep):
    rows = give.shape[2]
    t = lax.axis_index("tensor")
    x, c = t // 2, t % 2
    for j in range(nt):
        k, other = j % nx, j < nx
        place = lax.rem(x + k, nx) * 2 + ((1 - c) if other else c)
        source = pl.ds(pl.multiple_of(place * rows, rows), rows)
        to = give if other else keep
        to[k] = lax.dot_general(values[source], basis[...], (((1,), (1,)), ((), ())), preferred_element_type=F32).T


def project(values, basis, token, nt):
    rank, hidden = basis.shape
    rows = values.shape[0] // nt
    nx = nt // 2
    shape = jax.ShapeDtypeStruct((nx, rank, rows), F32)
    return pl.pallas_call(
        functools.partial(project_kernel, nx, nt),
        out_shape=[shape, shape],
        in_specs=[pl.BlockSpec(memory_space=pltpu.VMEM)] * 3,
        out_specs=[pl.BlockSpec(memory_space=pltpu.VMEM)] * 2,
        compiler_params=pltpu.CompilerParams(vmem_limit_bytes=16 * 2**20),
        cost_estimate=pl.CostEstimate(flops=2 * nt * rows * hidden * rank, bytes_accessed=2 * nt * rows * hidden, transcendentals=0),
    )(values, basis, token)


def outer_kernel(nx, own, scale, keep, everyone, sketch):
    mine = keep[0]
    for k in range(1, nx):
        mine = mine + everyone[k - 1].astype(F32)
    rank, length = mine.shape[0] // 2, mine.shape[1] // own
    for s in range(own):
        part = mine[:, s * length : (s + 1) * length]
        sketch[s] = scale * lax.dot_general(
            part[:rank], part[rank:], (((1,), (1,)), ((), ())), precision=lax.Precision.HIGHEST, preferred_element_type=F32
        )


def outer(keep, everyone, own):
    nx, twice, tokens = keep.shape
    rank = twice // 2
    return pl.pallas_call(
        functools.partial(outer_kernel, nx, own, 1.0 / (tokens // own * rank)),
        out_shape=jax.ShapeDtypeStruct((own, rank, rank), F32),
        in_specs=[pl.BlockSpec(memory_space=pltpu.VMEM)] * 2,
        out_specs=pl.BlockSpec(memory_space=pltpu.VMEM),
        compiler_params=pltpu.CompilerParams(vmem_limit_bytes=16 * 2**20),
        cost_estimate=pl.CostEstimate(flops=12 * rank * rank * tokens, bytes_accessed=4 * keep.size, transcendentals=0),
    )(keep, everyone)


def score_kernel(no, own, outer_axis, rows, near, mine, other, out):
    c = lax.axis_index("tensor") % 2
    value = rows[...]
    hi = value.astype(BF).astype(F32)
    split = jnp.concatenate([hi, value - hi], 0).astype(BF)
    d = lax.axis_index("dp")
    i = d % 2 if outer_axis else d // no

    def product(q):
        return lax.dot_general(split, q[...], (((1,), (1,)), ((), ())), preferred_element_type=F32)

    n, m, f = product(near), product(mine), product(other)
    far = jnp.where(c == 0, jnp.concatenate([m, f], 1), jnp.concatenate([f, m], 1))
    every = jnp.where(i == 0, jnp.concatenate([n, far], 1), jnp.concatenate([far, n], 1))
    for k in range(no):
        out[k] = every[own * k : own * (k + 1)] + every[own * (no + k) : own * (no + k + 1)]


def score(rows, near, mine, other, no, own, outer_axis):
    return pl.pallas_call(
        functools.partial(score_kernel, no, own, outer_axis),
        out_shape=jax.ShapeDtypeStruct((no, own, 2 * near.shape[0]), F32),
        in_specs=[pl.BlockSpec(memory_space=pltpu.VMEM)] * 4,
        out_specs=pl.BlockSpec(memory_space=pltpu.VMEM),
        compiler_params=pltpu.CompilerParams(vmem_limit_bytes=16 * 2**20),
        cost_estimate=pl.CostEstimate(flops=8 * rows.size * near.shape[0], bytes_accessed=2 * near.size, transcendentals=0),
    )(rows, near, mine, other)


def local(acts, grads, basis_in, basis_out, queries):
    rank = basis_in.shape[0]
    length, hidden = acts.shape[1:]
    nt, nd = lax.axis_size("tensor"), lax.axis_size("dp")
    nx, no = nt // 2, nd // 2
    t, d = lax.axis_index("tensor"), lax.axis_index("dp")
    c = t % 2
    o, i = d // 2, d % 2

    def at(a, b):
        return a * 2 + b

    own = acts.shape[0] // nt
    nq = queries.shape[0]
    core = [(k, k ^ 1) for k in range(nt)]

    def xshift(k):
        return [(a * 2 + b, ((a + k) % nx) * 2 + b) for a in range(nx) for b in range(2)]

    def oshift(k):
        return [(at(a, b), at((a + k) % no, b)) for a in range(no) for b in range(2)]

    near = [(at(a, b), at(a, 1 - b)) for a in range(no) for b in range(2)]

    half = nq // 2
    part = lax.dynamic_slice_in_dim(queries, c * half, half, 0)
    token = opening()
    far_mine = lax.ppermute(part, "dp", near)
    x = t // 2
    pairs = [[a * 2, a * 2 + 1] for a in range(nx)]
    columns = [[a * 2 + b for a in range(nx)] for b in range(2)]
    outers = [[at(a, b) for a in range(no)] for b in range(2)]

    def swap(value):
        return lax.dynamic_index_in_dim(lax.all_gather(value, "tensor", axis=0, axis_index_groups=pairs), 1 - c, 0, False)

    give_r, keep_r = project(grads.reshape(-1, hidden), basis_out, token, nt)
    give_l, keep_l = project(acts.reshape(-1, hidden), basis_in, token, nt)
    got = lax.ppermute(jnp.concatenate([give_l, give_r], 1), "tensor", core)
    keep = jnp.concatenate([keep_l, keep_r], 1) + got
    arrived = [lax.ppermute(keep[k].astype(BF), "tensor", xshift(k)) for k in range(1, nx)]
    everyone = jnp.stack(arrived, 0)
    rows = outer(keep, everyone, own).reshape(own, rank * rank)
    stacked = jnp.concatenate([rows] + [lax.ppermute(rows, "dp", oshift(k)) for k in range(1, no)], 0)
    far_other = lax.ppermute(far_mine, "tensor", core)

    def back(s):
        return [s[0]] + [lax.ppermute(s[k], "dp", oshift(no - k)) for k in range(1, no)]
    allb = jnp.stack(back(score(stacked, queries, far_mine, far_other, no, own, True)), 0)
    allb = jnp.roll(allb, o, axis=0) if no > 2 else jnp.where(o == 0, allb, allb[::-1])
    return jnp.swapaxes(allb, 0, 1).reshape(own, nd * nq)


def solution(mesh):
    in_specs = (
        P(("groups", "dp"), None, "tensor"),
        P(("groups", "dp"), None, "tensor"),
        P(None, "tensor"),
        P(None, "tensor"),
        P(("groups", "dp"), None),
    )
    out_specs = P(("groups", "dp", "tensor"), None)
    return jax.shard_map(local, mesh=mesh, in_specs=in_specs, out_specs=out_specs, check_vma=False)
```

```python
import functools

import jax
import jax.numpy as jnp
from jax import lax
from jax.experimental import pallas as pl
from jax.experimental.pallas import tpu as pltpu
from jax.sharding import PartitionSpec as P

BF, F32 = jnp.bfloat16, jnp.float32


def open_kernel(token):
    token[...] = jnp.zeros_like(token)


def opening():
    return pl.pallas_call(
        open_kernel,
        out_shape=jax.ShapeDtypeStruct((8, 128), F32),
        out_specs=pl.BlockSpec(memory_space=pltpu.VMEM),
        compiler_params=pltpu.CompilerParams(vmem_limit_bytes=4 * 2**20),
        cost_estimate=pl.CostEstimate(flops=10000000000, bytes_accessed=0, transcendentals=0),
    )()


def project_kernel(nx, nt, values, basis, token, *refs):
    give, keep = refs[-2:]
    rank, rows = basis.shape[0], give.shape[2]
    if len(refs) > 2:
        give[:, rank:] = refs[0][...]
        keep[:, rank:] = refs[1][...]
    t = lax.axis_index("tensor")
    x, c = t // 2, t % 2
    for j in range(nt):
        k, other = j % nx, j < nx
        place = lax.rem(x + k, nx) * 2 + ((1 - c) if other else c)
        source = pl.ds(pl.multiple_of(place * rows, rows), rows)
        to = give if other else keep
        to[k, :rank] = lax.dot_general(values[source], basis[...], (((1,), (1,)), ((), ())), preferred_element_type=F32).T


def project(values, basis, token, nt, *others):
    rank, hidden = basis.shape
    rows = values.shape[0] // nt
    nx = nt // 2
    shape = jax.ShapeDtypeStruct((nx, 2 * rank if others else rank, rows), F32)
    return pl.pallas_call(
        functools.partial(project_kernel, nx, nt),
        out_shape=[shape, shape],
        in_specs=[pl.BlockSpec(memory_space=pltpu.VMEM)] * (3 + len(others)),
        out_specs=[pl.BlockSpec(memory_space=pltpu.VMEM)] * 2,
        compiler_params=pltpu.CompilerParams(vmem_limit_bytes=4 * 2**20),
        cost_estimate=pl.CostEstimate(flops=2 * nt * rows * hidden * rank, bytes_accessed=2 * nt * rows * hidden, transcendentals=0),
    )(values, basis, token, *others)


def outer_kernel(nx, own, scale, keep, everyone, sketch):
    mine = keep[0]
    for k in range(1, nx):
        mine = mine + everyone[k - 1].astype(F32)
    rank, length = mine.shape[0] // 2, mine.shape[1] // own
    for s in range(own):
        part = mine[:, s * length : (s + 1) * length]
        sketch[s] = scale * lax.dot_general(
            part[:rank], part[rank:], (((1,), (1,)), ((), ())), precision=lax.Precision.HIGHEST, preferred_element_type=F32
        )


def outer(keep, everyone, own):
    nx, twice, tokens = keep.shape
    rank = twice // 2
    return pl.pallas_call(
        functools.partial(outer_kernel, nx, own, 1.0 / (tokens // own * rank)),
        out_shape=jax.ShapeDtypeStruct((own, rank, rank), F32),
        in_specs=[pl.BlockSpec(memory_space=pltpu.VMEM)] * 2,
        out_specs=pl.BlockSpec(memory_space=pltpu.VMEM),
        compiler_params=pltpu.CompilerParams(vmem_limit_bytes=4 * 2**20),
        cost_estimate=pl.CostEstimate(flops=12 * rank * rank * tokens, bytes_accessed=4 * keep.size, transcendentals=0),
    )(keep, everyone)


def score_kernel(no, own, outer_axis, rows, near, mine, other, out):
    c = lax.axis_index("tensor") % 2
    value = rows[...]
    hi = value.astype(BF).astype(F32)
    split = jnp.concatenate([hi, value - hi], 0).astype(BF)
    d = lax.axis_index("dp")
    i = d % 2 if outer_axis else d // no

    def product(q):
        return lax.dot_general(split, q[...], (((1,), (1,)), ((), ())), preferred_element_type=F32)

    n, m, f = product(near), product(mine), product(other)
    far = jnp.where(c == 0, jnp.concatenate([m, f], 1), jnp.concatenate([f, m], 1))
    every = jnp.where(i == 0, jnp.concatenate([n, far], 1), jnp.concatenate([far, n], 1))
    for k in range(no):
        out[k] = every[own * k : own * (k + 1)] + every[own * (no + k) : own * (no + k + 1)]


def score(rows, near, mine, other, no, own, outer_axis):
    return pl.pallas_call(
        functools.partial(score_kernel, no, own, outer_axis),
        out_shape=jax.ShapeDtypeStruct((no, own, 2 * near.shape[0]), F32),
        in_specs=[pl.BlockSpec(memory_space=pltpu.VMEM)] * 4,
        out_specs=pl.BlockSpec(memory_space=pltpu.VMEM),
        compiler_params=pltpu.CompilerParams(vmem_limit_bytes=4 * 2**20),
        cost_estimate=pl.CostEstimate(flops=8 * rows.size * near.shape[0], bytes_accessed=2 * near.size, transcendentals=0),
    )(rows, near, mine, other)


def local(acts, grads, basis_in, basis_out, queries):
    rank = basis_in.shape[0]
    length, hidden = acts.shape[1:]
    nt, nd = lax.axis_size("tensor"), lax.axis_size("dp")
    nx, no = nt // 2, nd // 2
    t, d = lax.axis_index("tensor"), lax.axis_index("dp")
    c = t % 2
    o, i = d // 2, d % 2

    def at(a, b):
        return a * 2 + b

    own = acts.shape[0] // nt
    nq = queries.shape[0]
    core = [(k, k ^ 1) for k in range(nt)]

    def xshift(k):
        return [(a * 2 + b, ((a + k) % nx) * 2 + b) for a in range(nx) for b in range(2)]

    def oshift(k):
        return [(at(a, b), at((a + k) % no, b)) for a in range(no) for b in range(2)]

    near = [(at(a, b), at(a, 1 - b)) for a in range(no) for b in range(2)]

    half = nq // 2
    part = lax.dynamic_slice_in_dim(queries, c * half, half, 0)
    token = opening()
    far_mine = lax.ppermute(part, "dp", near)
    x = t // 2
    pairs = [[a * 2, a * 2 + 1] for a in range(nx)]
    columns = [[a * 2 + b for a in range(nx)] for b in range(2)]
    outers = [[at(a, b) for a in range(no)] for b in range(2)]

    def swap(value):
        return lax.dynamic_index_in_dim(lax.all_gather(value, "tensor", axis=0, axis_index_groups=pairs), 1 - c, 0, False)

    give, keep = project(grads.reshape(-1, hidden), basis_out, token, nt)
    give, keep = project(acts.reshape(-1, hidden), basis_in, token, nt, give, keep)
    got = lax.ppermute(give, "tensor", core)
    keep = keep + got
    arrived = [lax.ppermute(keep[k].astype(BF), "tensor", xshift(k)) for k in range(1, nx)]
    everyone = jnp.stack(arrived, 0)
    rows = outer(keep, everyone, own).reshape(own, rank * rank)
    stacked = jnp.concatenate([rows] + [lax.ppermute(rows, "dp", oshift(k)) for k in range(1, no)], 0)
    far_other = lax.ppermute(far_mine, "tensor", core)

    def back(s):
        return [s[0]] + [lax.ppermute(s[k], "dp", oshift(no - k)) for k in range(1, no)]
    allb = jnp.stack(back(score(stacked, queries, far_mine, far_other, no, own, True)), 0)
    allb = jnp.roll(allb, o, axis=0) if no > 2 else jnp.where(o == 0, allb, allb[::-1])
    return jnp.swapaxes(allb, 0, 1).reshape(own, nd * nq)


def solution(mesh):
    in_specs = (
        P(("groups", "dp"), None, "tensor"),
        P(("groups", "dp"), None, "tensor"),
        P(None, "tensor"),
        P(None, "tensor"),
        P(("groups", "dp"), None),
    )
    out_specs = P(("groups", "dp", "tensor"), None)
    return jax.shard_map(local, mesh=mesh, in_specs=in_specs, out_specs=out_specs, check_vma=False)
```

```python
import functools

import jax
import jax.numpy as jnp
from jax import lax
from jax.experimental import pallas as pl
from jax.experimental.pallas import tpu as pltpu
from jax.sharding import PartitionSpec as P

BF, F32 = jnp.bfloat16, jnp.float32


def open_kernel(token):
    token[...] = jnp.zeros_like(token)


def opening():
    return pl.pallas_call(
        open_kernel,
        out_shape=jax.ShapeDtypeStruct((8, 128), F32),
        out_specs=pl.BlockSpec(memory_space=pltpu.VMEM),
        compiler_params=pltpu.CompilerParams(vmem_limit_bytes=4 * 2**20),
        cost_estimate=pl.CostEstimate(flops=10000000000, bytes_accessed=0, transcendentals=0),
    )()


def project_kernel(nx, nt, values, basis, token, *refs):
    give, keep = refs[-2:]
    rank, rows = basis.shape[0], give.shape[2]
    if len(refs) > 2:
        give[:, rank:] = refs[0][...]
        keep[:, rank:] = refs[1][...]
    t = lax.axis_index("tensor")
    x, c = t // 2, t % 2
    for j in range(nt):
        k, other = j % nx, j < nx
        place = lax.rem(x + k, nx) * 2 + ((1 - c) if other else c)
        source = pl.ds(pl.multiple_of(place * rows, rows), rows)
        to = give if other else keep
        to[k, :rank] = lax.dot_general(values[source], basis[...], (((1,), (1,)), ((), ())), preferred_element_type=F32).T


def project(values, basis, token, nt, *others):
    rank, hidden = basis.shape
    rows = values.shape[0] // nt
    nx = nt // 2
    shape = jax.ShapeDtypeStruct((nx, 2 * rank if others else rank, rows), F32)
    return pl.pallas_call(
        functools.partial(project_kernel, nx, nt),
        out_shape=[shape, shape],
        in_specs=[pl.BlockSpec(memory_space=pltpu.VMEM)] * (3 + len(others)),
        out_specs=[pl.BlockSpec(memory_space=pltpu.VMEM)] * 2,
        compiler_params=pltpu.CompilerParams(vmem_limit_bytes=4 * 2**20),
        cost_estimate=pl.CostEstimate(flops=2 * nt * rows * hidden * rank, bytes_accessed=2 * nt * rows * hidden, transcendentals=0),
    )(values, basis, token, *others)


def outer_kernel(nx, own, scale, keep, got, everyone, sketch):
    mine = keep[0] + got[0]
    for k in range(1, nx):
        mine = mine + everyone[k - 1].astype(F32)
    rank, length = mine.shape[0] // 2, mine.shape[1] // own
    for s in range(own):
        part = mine[:, s * length : (s + 1) * length]
        sketch[s] = scale * lax.dot_general(
            part[:rank], part[rank:], (((1,), (1,)), ((), ())), precision=lax.Precision.HIGHEST, preferred_element_type=F32
        )


def outer(keep, got, everyone, own):
    nx, twice, tokens = keep.shape
    rank = twice // 2
    return pl.pallas_call(
        functools.partial(outer_kernel, nx, own, 1.0 / (tokens // own * rank)),
        out_shape=jax.ShapeDtypeStruct((own, rank, rank), F32),
        in_specs=[pl.BlockSpec(memory_space=pltpu.VMEM)] * 3,
        out_specs=pl.BlockSpec(memory_space=pltpu.VMEM),
        compiler_params=pltpu.CompilerParams(vmem_limit_bytes=4 * 2**20),
        cost_estimate=pl.CostEstimate(flops=12 * rank * rank * tokens, bytes_accessed=4 * keep.size, transcendentals=0),
    )(keep, got, everyone)


def score_kernel(no, own, outer_axis, rows, near, mine, other, out):
    c = lax.axis_index("tensor") % 2
    value = rows[...]
    hi = value.astype(BF).astype(F32)
    split = jnp.concatenate([hi, value - hi], 0).astype(BF)
    d = lax.axis_index("dp")
    i = d % 2 if outer_axis else d // no

    def product(q):
        return lax.dot_general(split, q[...], (((1,), (1,)), ((), ())), preferred_element_type=F32)

    n, m, f = product(near), product(mine), product(other)
    far = jnp.where(c == 0, jnp.concatenate([m, f], 1), jnp.concatenate([f, m], 1))
    every = jnp.where(i == 0, jnp.concatenate([n, far], 1), jnp.concatenate([far, n], 1))
    for k in range(no):
        out[k] = every[own * k : own * (k + 1)] + every[own * (no + k) : own * (no + k + 1)]


def score(rows, near, mine, other, no, own, outer_axis):
    return pl.pallas_call(
        functools.partial(score_kernel, no, own, outer_axis),
        out_shape=jax.ShapeDtypeStruct((no, own, 2 * near.shape[0]), F32),
        in_specs=[pl.BlockSpec(memory_space=pltpu.VMEM)] * 4,
        out_specs=pl.BlockSpec(memory_space=pltpu.VMEM),
        compiler_params=pltpu.CompilerParams(vmem_limit_bytes=4 * 2**20),
        cost_estimate=pl.CostEstimate(flops=8 * rows.size * near.shape[0], bytes_accessed=2 * near.size, transcendentals=0),
    )(rows, near, mine, other)


def local(acts, grads, basis_in, basis_out, queries):
    rank = basis_in.shape[0]
    length, hidden = acts.shape[1:]
    nt, nd = lax.axis_size("tensor"), lax.axis_size("dp")
    nx, no = nt // 2, nd // 2
    t, d = lax.axis_index("tensor"), lax.axis_index("dp")
    c = t % 2
    o, i = d // 2, d % 2

    def at(a, b):
        return a * 2 + b

    own = acts.shape[0] // nt
    nq = queries.shape[0]
    core = [(k, k ^ 1) for k in range(nt)]

    def xshift(k):
        return [(a * 2 + b, ((a + k) % nx) * 2 + b) for a in range(nx) for b in range(2)]

    def oshift(k):
        return [(at(a, b), at((a + k) % no, b)) for a in range(no) for b in range(2)]

    near = [(at(a, b), at(a, 1 - b)) for a in range(no) for b in range(2)]

    half = nq // 2
    part = lax.dynamic_slice_in_dim(queries, c * half, half, 0)
    token = opening()
    far_mine = lax.ppermute(part, "dp", near)
    x = t // 2
    pairs = [[a * 2, a * 2 + 1] for a in range(nx)]
    columns = [[a * 2 + b for a in range(nx)] for b in range(2)]
    outers = [[at(a, b) for a in range(no)] for b in range(2)]

    def swap(value):
        return lax.dynamic_index_in_dim(lax.all_gather(value, "tensor", axis=0, axis_index_groups=pairs), 1 - c, 0, False)

    give, keep = project(grads.reshape(-1, hidden), basis_out, token, nt)
    give, keep = project(acts.reshape(-1, hidden), basis_in, token, nt, give, keep)
    got = lax.ppermute(give, "tensor", core)
    arrived = [lax.ppermute((keep[k] + got[k]).astype(BF), "tensor", xshift(k)) for k in range(1, nx)]
    everyone = jnp.stack(arrived, 0)
    rows = outer(keep, got, everyone, own).reshape(own, rank * rank)
    stacked = jnp.concatenate([rows] + [lax.ppermute(rows, "dp", oshift(k)) for k in range(1, no)], 0)
    far_other = lax.ppermute(far_mine, "tensor", core)

    def back(s):
        return [s[0]] + [lax.ppermute(s[k], "dp", oshift(no - k)) for k in range(1, no)]
    allb = jnp.stack(back(score(stacked, queries, far_mine, far_other, no, own, True)), 0)
    allb = jnp.roll(allb, o, axis=0) if no > 2 else jnp.where(o == 0, allb, allb[::-1])
    return jnp.swapaxes(allb, 0, 1).reshape(own, nd * nq)


def solution(mesh):
    in_specs = (
        P(("groups", "dp"), None, "tensor"),
        P(("groups", "dp"), None, "tensor"),
        P(None, "tensor"),
        P(None, "tensor"),
        P(("groups", "dp"), None),
    )
    out_specs = P(("groups", "dp", "tensor"), None)
    return jax.shard_map(local, mesh=mesh, in_specs=in_specs, out_specs=out_specs, check_vma=False)
```
